512 devices in a mesh: layer: 16 (over z), leaf: 32 (over y, x, core).
Axes of the slice: x: 4, y: 4, z: 16, core: 2. Of those that a mesh axis runs over, the one named last changes fastest.
Arguments:
- right_side: bfloat16 [16, 2, 32, 32768], P('layer', None, None, 'leaf'), may hold values from -6 to 6
- near_blocks: bfloat16 [16, 3, 2, 32768, 256], P('layer', None, None, 'leaf'), may hold values from -0.21875 to 0.21875
- right_bases: bfloat16 [16, 2, 2, 16, 32768], P('layer', None, None, None, 'leaf'), may hold values from -0.0625 to 0.0625
- left_bases: bfloat16 [16, 2, 2, 16, 32768], P('layer', None, None, None, 'leaf'), may hold values from -1 to 1
- coupling: bfloat16 [16, 32768], P('layer', 'leaf'), may hold values from 0.25 to 0.69921875
- ranks: int32 [16, 6], P('layer'), may hold values from 8 to 16
Outputs:
- swept: bfloat16 [16, 2, 32, 32768], P('layer', None, None, 'leaf')
The draws below stay inside these ranges and needn't reach their ends.
Inputs may be any that keep to these rules, and one draw needn't show every extreme that they name: ranks[k, s] is the rank in use of layer k's far block that maps into cluster s at level 0 (s = 0, 1) or cluster s - 2 at level 1 (s = 2 to 5).
All inputs are finite; a program needn't handle non-finite values.
Results may differ from the reference program's by a relative error of at most 0.035.
Values may be sent and summed in bfloat16 or wider, within the bound.
No kernel may reach another device: no remote copies, remote signals or barrier semaphores. Data moves between devices by JAX's collectives and lax.ppermute only.
A program may use at most 64 MiB of HBM per device.

```python
import math
import jax
import jax.numpy as jnp
from jax import lax

CELLS = 256
RANK = 16
RHS = 32
PLANE = 32768
N_LAYER = 16


def touch_ends(drawn, stream_key, low, top_value):
    place = [jax.random.randint(jax.random.fold_in(stream_key, axis), (), 0, length) for axis, length in enumerate(drawn.shape)]
    longest = drawn.shape.index(max(drawn.shape))
    next_to = place[:longest] + [(place[longest] + 1) % drawn.shape[longest]] + place[longest + 1:]
    return drawn.at[tuple(place)].set(low).at[tuple(next_to)].set(top_value)


def levels(own_key, dims, shards, low, largest):
    gain = 1.0
    for position, blocks in shards:
        draws = jax.random.uniform(jax.random.fold_in(jax.random.fold_in(own_key, 6), position), (blocks,), jnp.float32, low / len(shards), largest / len(shards))
        gain = gain * jnp.repeat(jnp.exp(draws), dims[position] // blocks).reshape((-1,) + (1,) * (len(dims) - 1 - position))
    return gain


def centred(own_key, extent, spread, limit, shards=(), held_as=jnp.bfloat16):
    factor_of = levels(own_key, extent, shards, -0.22, 0.18) if shards else 1.0
    array = jax.random.normal(own_key, extent, jnp.float32) * spread * factor_of
    return jnp.minimum(jnp.maximum(array, -limit), limit).astype(held_as)


def setup_inputs(seed: int = 0) -> dict:
    key_list = jax.random.split(jax.random.key(seed), 7)
    return {
        "right_side": centred(key_list[0], (N_LAYER, 2, RHS, PLANE), 1.0, 6.0, ((0, 16), (3, 32))),
        "near_blocks": centred(key_list[1], (N_LAYER, 3, 2, PLANE, CELLS), (3 * CELLS) ** -0.5, 0.21875, ((0, 16), (3, 32))),
        "right_bases": centred(key_list[2], (N_LAYER, 2, 2, RANK, PLANE), (PLANE // 4) ** -0.5, 0.0625, ((0, 16), (4, 32))),
        "left_bases": centred(key_list[3], (N_LAYER, 2, 2, RANK, PLANE), (2 * RANK) ** -0.5, 1.0, ((0, 16), (4, 32))),
        "coupling": jnp.clip(jnp.exp(math.log(0.69921875) - 1.0285027 * jax.random.uniform(key_list[4], (N_LAYER, PLANE), jnp.float32) ** levels(key_list[4], (N_LAYER, PLANE), ((0, 16), (1, 32)), -0.2, 0.2)), 0.25, 0.69921875).astype(jnp.bfloat16),
        "ranks": touch_ends(jax.random.randint(key_list[5], (N_LAYER, 6), RANK // 2, RANK + 1), jax.random.fold_in(key_list[5], 1), RANK // 2, RANK).astype(jnp.int32),
    }


def complex_rows(first, second, form):
    real_part = jnp.einsum(form, first[0], second[0]) - jnp.einsum(form, first[1], second[1])
    imag_part = jnp.einsum(form, first[0], second[1]) + jnp.einsum(form, first[1], second[0])
    return jnp.stack([real_part, imag_part])


def near_term(field, blocks):
    lower_side = jnp.pad(field[:, :, :-1], ((0, 0), (0, 0), (1, 0), (0, 0)))
    upper_side = jnp.pad(field[:, :, 1:], ((0, 0), (0, 0), (0, 1), (0, 0)))
    form = "rnp,nqp->rnq"
    total = complex_rows(field, blocks[0], form)
    total = total + complex_rows(lower_side, blocks[1], form)
    return total + complex_rows(upper_side, blocks[2], form)


def far_term(field, right_layer, left_layer, rank_row):
    total = jnp.zeros((2, RHS, PLANE), jnp.float32)
    for level, count in ((0, 2), (1, 4)):
        width = PLANE // count
        pieces = field.reshape(2, RHS, count, width)
        right_split = right_layer[level].reshape(2, RANK, count, width)
        coeff = complex_rows(pieces, right_split, "rcp,acp->rca")
        coeff = lax.optimization_barrier(coeff.astype(jnp.bfloat16)).astype(jnp.float32)
        swapped = coeff.reshape(2, RHS, count // 2, 2, RANK)[:, :, :, ::-1].reshape(2, RHS, count, RANK)
        limits = rank_row[2 * level:2 * level + count]
        keep = (jnp.arange(RANK)[None, :] < limits[:, None]).astype(jnp.float32)
        swapped = swapped * keep[None, None]
        left_split = left_layer[level].reshape(2, RANK, count, width)
        total = total + complex_rows(swapped, left_split, "rca,acp->rcp").reshape(2, RHS, PLANE)
    return total


def apply_inverse(layer_id, field_low, near_blocks, right_bases, left_bases, ranks):
    leaf_total = PLANE // CELLS
    field = field_low.astype(jnp.float32)
    blocks = near_blocks[layer_id].astype(jnp.float32).reshape(3, 2, leaf_total, CELLS, CELLS)
    near_value = near_term(field.reshape(2, RHS, leaf_total, CELLS), blocks).reshape(2, RHS, PLANE)
    far_value = far_term(field, right_bases[layer_id].astype(jnp.float32), left_bases[layer_id].astype(jnp.float32), ranks[layer_id])
    return near_value + far_value


def reference(right_side, near_blocks, right_bases, left_bases, coupling, ranks):
    def solve(layer_id, field_low):
        return apply_inverse(layer_id, field_low, near_blocks, right_bases, left_bases, ranks)

    inner = [solve(layer_id, right_side[layer_id]) for layer_id in range(N_LAYER)]
    forward = [inner[0].astype(jnp.bfloat16)]
    for layer_id in range(1, N_LAYER):
        coupled = (coupling[layer_id - 1].astype(jnp.float32) * forward[layer_id - 1].astype(jnp.float32)).astype(jnp.bfloat16)
        forward.append((inner[layer_id] - solve(layer_id, coupled)).astype(jnp.bfloat16))
    return jnp.stack(forward)
```

```python
import functools

import jax
import jax.numpy as jnp
from jax import lax
from jax.experimental import pallas as pl
from jax.experimental.pallas import tpu as pltpu
from jax.sharding import PartitionSpec as P

CELLS = 256
ROWS = 64
HALF = 32
LANES = 128
BF16 = jnp.bfloat16
F32 = jnp.float32
GRANT = 24 * 1024 * 1024


def row_dot(first, second):
    return lax.dot_general(first, second, (((1,), (1,)), ((), ())), preferred_element_type=F32)


def mat_dot(first, second):
    return jnp.dot(first, second, preferred_element_type=F32)


def turned(field):
    return jnp.concatenate([-field[HALF:], field[:HALF]], axis=0)


def coefficients(field, right):
    return row_dot(field[:HALF], right) + row_dot(field[HALF:], turned(right))


def packed(coeff):
    return jnp.concatenate([coeff[:16], coeff[16:]], axis=1)


def unpacked(dense):
    return jnp.concatenate([dense[:, :ROWS], dense[:, ROWS:]], axis=0)


def by_quarter(sums):
    return jnp.concatenate([unpacked(sums[q]) for q in range(4)], axis=1)


def seen(quarter, viewer):
    level = (lax.broadcasted_iota(jnp.int32, (ROWS, 1), 0) // 16) % 2
    far_half = jnp.where(viewer // 2 == quarter // 2, 0.0, 1.0).astype(F32)
    sibling = jnp.where(jnp.bitwise_xor(viewer, 1) == quarter, 1.0, 0.0).astype(F32)
    return jnp.where(level == 0, far_half, sibling)


def weights_of(basis):
    real, imag = basis[:HALF], basis[HALF:]
    return jnp.concatenate([real, -imag], axis=0), jnp.concatenate([imag, real], axis=0)


def far_rows(coeff, weights_ref):
    width = weights_ref.shape[1] // 2
    both = mat_dot(coeff, weights_ref[...])
    return jnp.concatenate([both[:, :width], both[:, width:]], axis=0)


def near_leaf(leaf, leaves, own, lower, upper, blocks_ref, total=None):
    rows = slice(leaf * CELLS, (leaf + 1) * CELLS)
    below = own[leaf - 1] if leaf else lower
    above = own[leaf + 1] if leaf + 1 < leaves else upper
    for side, part in ((0, own[leaf]), (1, below), (2, above)):
        if part is None:
            continue
        term = row_dot(part, blocks_ref[side, 0, rows, :])
        term = term + row_dot(turned(part), blocks_ref[side, 1, rows, :])
        total = term if total is None else total + term
    return total


def first_kernel(field, lower, upper, basis, basis_low, basis_up, blocks, right, near, ext, ext_low, ext_up, sums):
    width = field.shape[1]
    leaves = width // CELLS
    own_x = [field[:, j * CELLS : (j + 1) * CELLS] for j in range(leaves)]
    own_b = [basis[:, j * CELLS : (j + 1) * CELLS] for j in range(leaves)]
    for j in range(leaves):
        cols = slice(j * CELLS, (j + 1) * CELLS)
        near[:, cols] = near_leaf(j, leaves, own_x, lower[...], upper[...], blocks)
        ext[:, cols] = near_leaf(j, leaves, own_b, None, None, blocks)
    rows = slice(0, CELLS)
    edge = row_dot(basis_low[...], blocks[1, 0, rows, :])
    ext_low[...] = edge + row_dot(turned(basis_low[...]), blocks[1, 1, rows, :])
    rows = slice((leaves - 1) * CELLS, leaves * CELLS)
    edge = row_dot(basis_up[...], blocks[2, 0, rows, :])
    ext_up[...] = edge + row_dot(turned(basis_up[...]), blocks[2, 1, rows, :])
    sums[:16] = packed(coefficients(field[...], right[...])).astype(BF16)
    sums[16:] = packed(coefficients(basis[...], right[...])).astype(BF16)


def emit_field(value, coupling, right_next, carried, out, out_low, out_up, out_sums):
    width = value.shape[1]
    sent = (coupling * value).astype(BF16)
    out[:, :width] = sent
    out[:HALF, width:] = carried[:, :LANES]
    out[HALF:, width:] = carried[:, LANES:]
    out_low[...] = sent[:, :CELLS]
    out_up[...] = sent[:, width - CELLS :]
    out_sums[...] = packed(coefficients(sent, right_next)).astype(BF16)


def second_kernel(
    place, all_sums, near, left, ext, ext_low, ext_up, coupling, right_next,
    base, left_w, ext_w, carry_w, out, out_low, out_up, out_sums,
):
    width = near.shape[1]
    mine, low_view, up_view = place[1], place[2], place[3]
    left_r, left_i = weights_of(left[...].astype(F32))
    ext_r, ext_i = weights_of(ext[...])
    low_r, low_i = weights_of(ext_low[...])
    up_r, up_i = weights_of(ext_up[...])
    last = width - CELLS
    for q in range(4):
        rows = slice(q * ROWS, (q + 1) * ROWS)
        own_mask, low_mask, up_mask = seen(q, mine), seen(q, low_view), seen(q, up_view)
        for at, left_p, ext_p, low_p, up_p in ((0, left_r, ext_r, low_r, up_r), (width, left_i, ext_i, low_i, up_i)):
            left_w[rows, at : at + width] = (left_p * own_mask).astype(BF16)
            ext_m = ext_p * own_mask
            ext_w[rows, at : at + CELLS] = (ext_m[:, :CELLS] + low_p * low_mask).astype(BF16)
            ext_w[rows, at + CELLS : at + last] = ext_m[:, CELLS:last].astype(BF16)
            ext_w[rows, at + last : at + width] = (ext_m[:, last:] + up_p * up_mask).astype(BF16)
    sums = jnp.sum(all_sums[...].astype(F32).reshape(4, -1, HALF, LANES), axis=1)
    coeff = by_quarter(sums[:, :16]).astype(BF16)
    columns = []
    for q in range(4):
        real = unpacked(sums[q, 16:])
        imag = jnp.concatenate([-real[:, HALF:], real[:, :HALF]], axis=1)
        block = jnp.concatenate([real, imag], axis=0)
        columns.append(jnp.concatenate([block * seen(s, q) for s in range(4)], axis=0))
    carry_w[...] = jnp.concatenate(columns, axis=1).astype(BF16)
    value = near[...] + far_rows(coeff, left_w)
    base[...] = value
    emit_field(
        value, coupling[...], right_next[...], jnp.zeros((HALF, 2 * LANES), BF16), out, out_low, out_up, out_sums
    )


def turn_kernel(
    place, turn, field, lower, upper, all_sums, blocks, base, ext_w, carry_w, coupling, right_next, old_value, old_coeff,
    value_out, coeff_out, out, out_low, out_up, out_sums,
):
    @pl.when(place[0] == turn[0])
    def _():
        width = base.shape[1]
        leaves = width // CELLS
        sums = jnp.sum(all_sums[...].astype(F32).reshape(4, -1, 16, LANES), axis=1)
        carried = jnp.concatenate([field[:HALF, width:], field[HALF:, width:]], axis=1)
        coeff = (by_quarter(sums) - carried.astype(F32)).astype(BF16)
        coeff_out[...] = coeff
        own = [field[:, j * CELLS : (j + 1) * CELLS] for j in range(leaves)]
        near = [near_leaf(j, leaves, own, lower[...], upper[...], blocks) for j in range(leaves)]
        value = base[...] - jnp.concatenate(near, axis=1) + far_rows(coeff, ext_w)
        value_out[...] = value
        onward = mat_dot(coeff, carry_w[...]).astype(BF16)
        emit_field(value, coupling[...], right_next[...], onward, out, out_low, out_up, out_sums)

    @pl.when(place[0] != turn[0])
    def _():
        value_out[...] = old_value[...]
        coeff_out[...] = old_coeff[...]


def last_kernel(place, layers, received, field, all_sums, value, left_w, out):
    width = value.shape[1]
    sums = jnp.sum(all_sums[...].astype(F32).reshape(4, -1, 16, LANES), axis=1)
    coeff = received[...]
    carried = jnp.concatenate([field[:HALF, width:], field[HALF:, width:]], axis=1).astype(F32)
    final = (by_quarter(sums) - carried).astype(BF16)
    coeff = jnp.where(place[0] == layers[0] - 1, final.astype(F32), coeff.astype(F32)).astype(BF16)
    out[...] = (value[...] - far_rows(coeff, left_w)).astype(BF16)


def vmem(count):
    return [pl.BlockSpec(memory_space=pltpu.VMEM)] * count


def smem(count):
    return [pl.BlockSpec(memory_space=pltpu.SMEM)] * count


def shape(dims, dtype):
    return jax.ShapeDtypeStruct(dims, dtype)


def body(right_side, near_blocks, right_bases, left_bases, coupling, ranks):
    layer_count = lax.axis_size("layer")
    leaf_count = lax.axis_size("leaf")
    layer = lax.axis_index("layer")
    leaf = lax.axis_index("leaf")
    width = right_side.shape[3]
    field = right_side[0].reshape(ROWS, width)
    blocks = near_blocks[0]
    own_coupling = coupling[0].astype(F32).reshape(1, width)
    right = right_bases[0].transpose(1, 0, 2, 3).reshape(ROWS, width)
    per_quarter = leaf_count // 4
    mine = leaf // per_quarter
    place = jnp.stack([layer, mine, (leaf + per_quarter - 1) // per_quarter - 1, (leaf + 1) // per_quarter])
    place = place.astype(jnp.int32)
    rank_row = ranks[0]
    slots = jnp.arange(6)
    limits = jnp.stack(
        [jnp.sum(jnp.where(slots == mine // 2, rank_row, 0)), jnp.sum(jnp.where(slots == 2 + mine, rank_row, 0))]
    )
    keep = jnp.arange(16)[None, :] < limits[:, None]
    left = jnp.where(keep[:, None, :, None], left_bases[0], jnp.zeros((), BF16))
    left = left.transpose(1, 0, 2, 3).reshape(ROWS, width)
    basis = (left.astype(F32) * own_coupling).astype(BF16)

    def beside(value, by):
        return lax.ppermute(value, "leaf", [(i, i + by) for i in range(leaf_count) if 0 <= i + by < leaf_count])

    def back(value):
        return lax.ppermute(value, "layer", [(i + 1, i) for i in range(layer_count - 1)])

    def ahead(value, turn, by, hop=1):
        pairs = [
            (k * leaf_count + i, (k + hop) * leaf_count + i + by)
            for k in range(layer_count - hop)
            if (k - turn) % 3 == 0
            for i in range(leaf_count)
            if 0 <= i + by < leaf_count
        ]
        return lax.ppermute(value, ("layer", "leaf"), pairs)

    def all_ahead(value, by):
        pairs = [
            (k * leaf_count + i, (k + 1) * leaf_count + i + by)
            for k in range(layer_count - 1)
            for i in range(leaf_count)
            if 0 <= i + by < leaf_count
        ]
        return lax.ppermute(value, ("layer", "leaf"), pairs)

    def to_all(value):
        copies = jnp.broadcast_to(value, (leaf_count, *value.shape))
        return lax.all_to_all(copies, "leaf", split_axis=0, concat_axis=0, tiled=True)

    def to_all_of(turn, value):
        return lax.cond(
            layer == turn, to_all, lambda v: jnp.zeros((leaf_count, *v.shape), v.dtype), value
        )

    params = pltpu.CompilerParams(vmem_limit_bytes=GRANT)
    lower = beside(field[:, width - CELLS :], 1)
    upper = beside(field[:, :CELLS], -1)
    basis_in = all_ahead(basis, 0)
    basis_low = all_ahead(basis[:, width - CELLS :], 1)
    basis_up = all_ahead(basis[:, :CELLS], -1)
    right_next = back(right)
    near, ext, ext_low, ext_up, sums = pl.pallas_call(
        first_kernel,
        out_shape=[
            shape((ROWS, width), F32), shape((ROWS, width), F32), shape((ROWS, CELLS), F32),
            shape((ROWS, CELLS), F32), shape((HALF, LANES), BF16),
        ],
        in_specs=vmem(8), out_specs=vmem(5), compiler_params=params, name="first",
    )(field, lower, upper, basis_in, basis_low, basis_up, blocks, right)
    base, left_w, ext_w, carry_w, sent, sent_low, sent_up, sums = pl.pallas_call(
        second_kernel,
        out_shape=[
            shape((ROWS, width), F32), shape((256, 2 * width), BF16), shape((256, 2 * width), BF16),
            shape((256, 256), BF16), shape((ROWS, width + LANES), BF16), shape((ROWS, CELLS), BF16),
            shape((ROWS, CELLS), BF16), shape((16, LANES), BF16),
        ],
        in_specs=smem(1) + vmem(8), out_specs=vmem(8), compiler_params=params, name="second",
    )(place, to_all(sums), near, left, ext, ext_low, ext_up, own_coupling, right_next)

    value = base
    coeff = jnp.zeros((HALF, 256), BF16)
    no_sums = jnp.zeros((leaf_count, 16, LANES), BF16)
    early = None
    turn_call = pl.pallas_call(
        turn_kernel,
        out_shape=[
            shape((ROWS, width), F32), shape((HALF, 256), BF16), shape((ROWS, width + LANES), BF16),
            shape((ROWS, CELLS), BF16), shape((ROWS, CELLS), BF16), shape((16, LANES), BF16),
        ],
        in_specs=smem(2) + vmem(12), out_specs=vmem(6), input_output_aliases={12: 0, 13: 1},
        compiler_params=params, name="turn",
    )
    for turn in range(1, layer_count):
        got = ahead(sent, turn - 1, 0)
        got_low = ahead(sent_up, turn - 1, 1)
        got_up = ahead(sent_low, turn - 1, -1)
        last_turn = turn == layer_count - 1
        next_early = ahead(sums, turn - 1, 0, 1 if last_turn else 2)
        summed = no_sums if early is None else to_all_of(turn, early)
        early = next_early
        value, coeff, sent, sent_low, sent_up, sums = turn_call(
            place, jnp.full((1,), turn, jnp.int32), got, got_low, got_up, summed, blocks, base, ext_w, carry_w,
            own_coupling, right_next, value, coeff,
        )
    summed = to_all_of(layer_count - 1, early)
    out = pl.pallas_call(
        last_kernel,
        out_shape=shape((ROWS, width), BF16),
        in_specs=smem(2) + vmem(5), out_specs=vmem(1)[0], compiler_params=params, name="last",
    )(place, jnp.full((1,), layer_count, jnp.int32), back(coeff), sent, summed, value, left_w)
    return out.reshape(2, HALF, width)[None]


def solution(mesh):
    placed = (
        P("layer", None, None, "leaf"),
        P("layer", None, None, "leaf", None),
        P("layer", None, None, None, "leaf"),
        P("layer", None, None, None, "leaf"),
        P("layer", "leaf"),
        P("layer", None),
    )
    return jax.shard_map(
        body, mesh=mesh, in_specs=placed, out_specs=P("layer", None, None, "leaf"), check_vma=False
    )
```

```python
import functools

import jax
import jax.numpy as jnp
from jax import lax
from jax.experimental import pallas as pl
from jax.experimental.pallas import tpu as pltpu
from jax.sharding import PartitionSpec as P

CELLS = 256
ROWS = 64
HALF = 32
SENT_ROWS = 144
LANES = 128
BF16 = jnp.bfloat16
F32 = jnp.float32
GRANT = 60 * 1024 * 1024


def row_dot(first, second):
    return lax.dot_general(first, second, (((1,), (1,)), ((), ())), preferred_element_type=F32)


def mat_dot(first, second):
    return jnp.dot(first, second, preferred_element_type=F32)


def turned(field):
    return jnp.concatenate([-field[HALF:], field[:HALF]], axis=0)


def coefficients(field, right):
    return row_dot(field[:HALF], right) + row_dot(field[HALF:], turned(right))


def packed(coeff):
    return jnp.concatenate([coeff[:16], coeff[16:]], axis=1)


def unpacked(dense):
    return jnp.concatenate([dense[:, :ROWS], dense[:, ROWS:]], axis=0)


def by_quarter(sums):
    return jnp.concatenate([unpacked(sums[q]) for q in range(4)], axis=1)


def seen(quarter, viewer):
    level = (lax.broadcasted_iota(jnp.int32, (ROWS, 1), 0) // 16) % 2
    far_half = jnp.where(viewer // 2 == quarter // 2, 0.0, 1.0).astype(F32)
    sibling = jnp.where(jnp.bitwise_xor(viewer, 1) == quarter, 1.0, 0.0).astype(F32)
    return jnp.where(level == 0, far_half, sibling)


def weights_of(basis):
    real, imag = basis[:HALF], basis[HALF:]
    return jnp.concatenate([real, -imag], axis=0), jnp.concatenate([imag, real], axis=0)


def far_rows(coeff, weights_ref):
    width = weights_ref.shape[1] // 2
    both = mat_dot(coeff, weights_ref[...])
    return jnp.concatenate([both[:, :width], both[:, width:]], axis=0)


def leaf_fetches(blocks_in, blocks, done):
    return [
        pltpu.make_async_copy(blocks_in.at[:, :, pl.ds(j * CELLS, CELLS)], blocks.at[j], done.at[j])
        for j in range(blocks.shape[0])
    ]


def near_leaf(leaf, leaves, own, lower, upper, blocks, total=None):
    below = own[leaf - 1] if leaf else lower
    above = own[leaf + 1] if leaf + 1 < leaves else upper
    for side, part in ((0, own[leaf]), (1, below), (2, above)):
        if part is None:
            continue
        term = row_dot(part, blocks[leaf, side, 0]) + row_dot(turned(part), blocks[leaf, side, 1])
        total = term if total is None else total + term
    return total


def own_quarter():
    per_quarter = lax.axis_size("leaf") // 4
    return lax.axis_index("leaf") // per_quarter


def prepare_kernel(ranks, field, left_parts, right_parts, coupling, left, basis, right, low_end, up_end):
    width = left.shape[1]
    mine = own_quarter()
    row = lax.broadcasted_iota(jnp.int32, (ROWS, 1), 0)
    limit = jnp.where((row // 16) % 2 == 0, ranks[0, mine // 2], ranks[0, 2 + mine])
    keep = jnp.where(row % 16 < limit, 1.0, 0.0).astype(F32)
    order = ((0, 0), (1, 0), (0, 1), (1, 1))
    stacked = jnp.concatenate([left_parts[level, part] for level, part in order], axis=0)
    kept = stacked.astype(F32) * keep
    left[...] = kept.astype(BF16)
    coupled = (kept * coupling[...].astype(F32)).astype(BF16)
    basis[...] = coupled
    right[...] = jnp.concatenate([right_parts[level, part] for level, part in order], axis=0)
    low_end[:ROWS] = field[:, :CELLS]
    low_end[ROWS:] = coupled[:, :CELLS]
    up_end[:ROWS] = field[:, width - CELLS :]
    up_end[ROWS:] = coupled[:, width - CELLS :]


def sums_kernel(field, basis, right, sums):
    sums[:16] = packed(coefficients(field[...], right[...])).astype(BF16)
    sums[16:] = packed(coefficients(basis[...], right[...])).astype(BF16)


def first_kernel(field, lower, upper, basis, ends, right_next, blocks_in, pack_out, pack, blocks, done):
    fetches = leaf_fetches(blocks_in, blocks, done)
    for fetch in fetches:
        fetch.start()
    width = field.shape[1]
    leaves = width // CELLS
    both = [
        jnp.concatenate([field[:, j * CELLS : (j + 1) * CELLS], basis[:, j * CELLS : (j + 1) * CELLS]], axis=0)
        for j in range(leaves)
    ]
    below = jnp.concatenate([lower[:ROWS], ends[:, :CELLS]], axis=0)
    above = jnp.concatenate([upper[:ROWS], ends[:, CELLS:]], axis=0)

    def product(part, leaf, side):
        spun = jnp.concatenate([turned(part[:ROWS]), turned(part[ROWS:])], axis=0)
        return row_dot(part, blocks[leaf, side, 0]) + row_dot(spun, blocks[leaf, side, 1])

    for j in range(leaves):
        fetches[j].wait()
        total = product(both[j], j, 0)
        for side, part, edge in (
            (1, both[j - 1] if j else below, j == 0), (2, both[j + 1] if j + 1 < leaves else above, j + 1 == leaves),
        ):
            term = product(part, j, side)
            if edge:
                at = 2 * width + (side - 1) * CELLS
                pack[:, at : at + CELLS] = term[ROWS:]
                term = jnp.concatenate([term[:ROWS], jnp.zeros((ROWS, CELLS), F32)], axis=0)
            total = total + term
        pack[:, j * CELLS : (j + 1) * CELLS] = total[:ROWS]
        pack[:, width + j * CELLS : width + (j + 1) * CELLS] = total[ROWS:]
    copy = pltpu.make_async_copy(pack, pack_out, done.at[leaves])
    copy.start()
    copy.wait()


def emit_field(value, coupling, right_next, carried, out, out_low, out_up, out_sums):
    width = value.shape[1]
    sent = (coupling * value).astype(BF16)
    out[:, :width] = sent
    out[:HALF, width:] = carried[:, :LANES]
    out[HALF:, width:] = carried[:, LANES:]
    out_low[...] = sent[:, :CELLS]
    out_up[...] = sent[:, width - CELLS :]
    out_sums[:16] = packed(coefficients(sent, right_next)).astype(BF16)


def second_kernel(
    all_sums, left, coupling, right_next, pack_in,
    value_out, base_out, left_out, weights_out, out, out_low, out_up, out_sums,
    pack, base, left_w, weights, done,
):
    fetch = pltpu.make_async_copy(pack_in, pack, done.at[0])
    fetch.start()
    width = left.shape[1]
    per_quarter = lax.axis_size("leaf") // 4
    leaf = lax.axis_index("leaf")
    mine = leaf // per_quarter
    low_view = (leaf + per_quarter - 1) // per_quarter - 1
    up_view = (leaf + 1) // per_quarter
    last = width - CELLS
    left_r, left_i = weights_of(left[...].astype(F32))
    for q in range(4):
        rows = slice(q * ROWS, (q + 1) * ROWS)
        own_mask = seen(q, mine)
        left_w[rows, :width] = (left_r * own_mask).astype(BF16)
        left_w[rows, width:] = (left_i * own_mask).astype(BF16)
    keep_left = pltpu.make_async_copy(left_w, left_out, done.at[1])
    keep_left.start()
    sums = jnp.sum(all_sums[...].astype(F32).reshape(4, -1, HALF, LANES), axis=1)
    coeff = by_quarter(sums[:, :16]).astype(BF16)
    far = far_rows(coeff, left_w)
    fetch.wait()
    value = pack[:, :width] + far
    base[:ROWS] = value
    base[ROWS:] = jnp.broadcast_to(coupling[...].astype(F32), (8, width))
    keep_base = pltpu.make_async_copy(base, base_out, done.at[2])
    keep_base.start()
    keep_value = pltpu.make_async_copy(base.at[:ROWS], value_out, done.at[3])
    keep_value.start()
    emit_field(
        value, coupling[...].astype(F32), right_next[...], jnp.zeros((HALF, 2 * LANES), BF16),
        out, out_low, out_up, out_sums,
    )
    ext_r, ext_i = weights_of(pack[:, width : 2 * width])
    low_r, low_i = weights_of(pack[:, 2 * width : 2 * width + CELLS])
    up_r, up_i = weights_of(pack[:, 2 * width + CELLS :])
    for q in range(4):
        rows = slice(q * ROWS, (q + 1) * ROWS)
        own_mask, low_mask, up_mask = seen(q, mine), seen(q, low_view), seen(q, up_view)
        for at, ext_p, low_p, up_p in ((0, ext_r, low_r, up_r), (width, ext_i, low_i, up_i)):
            ext_m = ext_p * own_mask
            weights[rows, at : at + CELLS] = (ext_m[:, :CELLS] + low_p * low_mask).astype(BF16)
            weights[rows, at + CELLS : at + last] = ext_m[:, CELLS:last].astype(BF16)
            weights[rows, at + last : at + width] = (ext_m[:, last:] + up_p * up_mask).astype(BF16)
    columns = []
    for q in range(4):
        real = unpacked(sums[q, 16:])
        imag = jnp.concatenate([-real[:, HALF:], real[:, :HALF]], axis=1)
        block = jnp.concatenate([real, imag], axis=0)
        columns.append(jnp.concatenate([block * seen(s, q) for s in range(4)], axis=0))
    weights[:, 2 * width :] = jnp.concatenate(columns, axis=1).astype(BF16)
    keep_weights = pltpu.make_async_copy(weights, weights_out, done.at[4])
    keep_weights.start()
    keep_left.wait()
    keep_base.wait()
    keep_value.wait()
    keep_weights.wait()


def turn_kernel(
    turn, field, lower, upper, all_sums, right_in, blocks_in, early, base_in, weights_in, old_value, old_coeff,
    value_out, coeff_out, field_out, low_out, up_out, sums_out,
    blocks, right_next, base, weights, value, coeff, sent, sent_low, sent_up, sent_sums, done,
):
    @pl.when(lax.axis_index("layer") == turn)
    def _():
        width = base.shape[1]
        leaves = width // CELLS
        leaf_parts = leaf_fetches(blocks_in, blocks, done)
        fetches = [
            pltpu.make_async_copy(source, target, done.at[leaves + number])
            for number, (source, target) in enumerate((
                (weights_in, weights), (base_in, base), (right_in, right_next),
            ))
        ]
        for fetch in leaf_parts + fetches:
            fetch.start()
        own = [field[:, j * CELLS : (j + 1) * CELLS] for j in range(leaves)]
        near = []
        for j in range(leaves):
            leaf_parts[j].wait()
            near.append(near_leaf(j, leaves, own, lower[...], upper[...], blocks))
        sums = jnp.sum(all_sums[...].astype(F32).reshape(4, -1, 16, LANES), axis=1)
        carried = jnp.concatenate([field[:HALF, width:], field[HALF:, width:]], axis=1)
        coeff[...] = (by_quarter(sums) - carried.astype(F32)).astype(BF16)
        fetches[0].wait()
        far = mat_dot(coeff[...], weights[...])
        fetches[1].wait()
        update = jnp.concatenate([far[:, :width], far[:, width : 2 * width]], axis=0)
        total = base[:ROWS] - jnp.concatenate(near, axis=1) + update
        value[...] = total
        onward = far[:, 2 * width :].astype(BF16)
        fetches[2].wait()
        emit_field(total, base[ROWS : ROWS + 1], right_next[...], onward, sent, sent_low, sent_up, sent_sums)
        keeps = [
            pltpu.make_async_copy(source, target, done.at[leaves + len(fetches) + number])
            for number, (source, target) in enumerate((
                (sent, field_out), (sent_low, low_out), (sent_up, up_out), (sent_sums, sums_out),
                (value, value_out), (coeff, coeff_out),
            ))
        ]
        for keep in keeps:
            keep.start()
        for keep in keeps:
            keep.wait()


def last_kernel(layers, received, all_sums, field_in, value_in, left_in, out, extras, value, left_w, done):
    width = value.shape[1]
    fetch_left = pltpu.make_async_copy(left_in, left_w, done.at[0])
    fetch_left.start()
    fetch_value = pltpu.make_async_copy(value_in, value, done.at[1])
    fetch_value.start()
    fetch_extras = pltpu.make_async_copy(field_in.at[:, width:], extras, done.at[2])
    fetch_extras.start()
    sums = jnp.sum(all_sums[...].astype(F32).reshape(4, -1, 16, LANES), axis=1)
    fetch_extras.wait()
    carried = jnp.concatenate([extras[:HALF], extras[HALF:]], axis=1).astype(F32)
    final = by_quarter(sums) - carried
    is_last = lax.axis_index("layer") == layers - 1
    coeff = jnp.where(is_last, final, received[...].astype(F32)).astype(BF16)
    fetch_left.wait()
    far = far_rows(coeff, left_w)
    fetch_value.wait()
    out[...] = (value[...] - far).astype(BF16)


def vmem(count):
    return [pl.BlockSpec(memory_space=pltpu.VMEM)] * count


def anywhere(count):
    return [pl.BlockSpec(memory_space=pl.ANY)] * count


def smem(count):
    return [pl.BlockSpec(memory_space=pltpu.SMEM)] * count


def shape(dims, dtype):
    return jax.ShapeDtypeStruct(dims, dtype)


def body(right_side, near_blocks, right_bases, left_bases, coupling, ranks):
    layer_count = lax.axis_size("layer")
    leaf_count = lax.axis_size("leaf")
    layer = lax.axis_index("layer")
    width = right_side.shape[3]
    field = right_side[0].reshape(ROWS, width)
    blocks = near_blocks[0]
    params = pltpu.CompilerParams(vmem_limit_bytes=GRANT)

    def beside(value, by):
        return lax.ppermute(value, "leaf", [(i, i + by) for i in range(leaf_count) if 0 <= i + by < leaf_count])

    def back(value):
        return lax.ppermute(value, "layer", [(i + 1, i) for i in range(layer_count - 1)])

    def ahead(value, turn, by, hop=1):
        pairs = [
            (k * leaf_count + i, (k + hop) * leaf_count + i + by)
            for k in range(layer_count - hop)
            if (k - turn) % 3 == 0
            for i in range(leaf_count)
            if 0 <= i + by < leaf_count
        ]
        return lax.ppermute(value, ("layer", "leaf"), pairs)

    def all_ahead(value, by):
        pairs = [
            (k * leaf_count + i, (k + 1) * leaf_count + i + by)
            for k in range(layer_count - 1)
            for i in range(leaf_count)
            if 0 <= i + by < leaf_count
        ]
        return lax.ppermute(value, ("layer", "leaf"), pairs)

    def to_all(value):
        copies = jnp.broadcast_to(value, (leaf_count, *value.shape))
        return lax.all_to_all(copies, "leaf", split_axis=0, concat_axis=0, tiled=True)

    def to_all_of(turn, value):
        return lax.cond(
            layer == turn, lambda v: to_all(v[:16]), lambda v: jnp.zeros((leaf_count, 16, LANES), v.dtype), value
        )

    left, basis, right, low_end, up_end = pl.pallas_call(
        prepare_kernel,
        out_shape=[shape((ROWS, width), BF16)] * 3 + [shape((2 * ROWS, CELLS), BF16)] * 2,
        in_specs=smem(1) + vmem(4), out_specs=vmem(5), compiler_params=params, name="prepare",
    )(ranks, field, left_bases[0], right_bases[0], coupling)
    lower = beside(up_end, 1)
    upper = beside(low_end, -1)
    basis_in = all_ahead(basis, 0)
    right_next = back(right)
    ends_in = all_ahead(jnp.concatenate([lower[ROWS:], upper[ROWS:]], axis=1), 0)
    sums = pl.pallas_call(
        sums_kernel, out_shape=shape((HALF, LANES), BF16),
        in_specs=vmem(3), out_specs=vmem(1)[0], compiler_params=params, name="sums",
    )(field, basis_in, right)
    all_sums = to_all(sums)
    packed_width = 2 * width + 2 * CELLS
    leaves = width // CELLS
    slabs_shape = (leaves, 3, 2, CELLS, CELLS)
    pack = pl.pallas_call(
        first_kernel,
        out_shape=shape((ROWS, packed_width), F32),
        in_specs=vmem(5) + anywhere(2), out_specs=anywhere(1)[0],
        scratch_shapes=[
            pltpu.VMEM((ROWS, packed_width), F32), pltpu.VMEM(slabs_shape, BF16), pltpu.SemaphoreType.DMA((leaves + 1,)),
        ],
        compiler_params=params, name="first",
    )(field, lower, upper, basis_in, ends_in, right_next, blocks)
    field_shapes = [
        shape((ROWS, width + LANES), BF16), shape((ROWS, CELLS), BF16), shape((ROWS, CELLS), BF16),
        shape((SENT_ROWS, LANES), BF16),
    ]
    base_shape, weights_shape = (ROWS + 8, width), (256, 2 * width + 256)
    value, base, left_w, weights, sent, sent_low, sent_up, sums = pl.pallas_call(
        second_kernel,
        out_shape=[
            shape((ROWS, width), F32), shape(base_shape, F32), shape((256, 2 * width), BF16),
            shape(weights_shape, BF16), *field_shapes,
        ],
        in_specs=vmem(4) + anywhere(1), out_specs=anywhere(4) + vmem(4),
        scratch_shapes=[
            pltpu.VMEM((ROWS, packed_width), F32), pltpu.VMEM(base_shape, F32), pltpu.VMEM((256, 2 * width), BF16),
            pltpu.VMEM(weights_shape, BF16), pltpu.SemaphoreType.DMA((5,)),
        ],
        compiler_params=params, name="second",
    )(all_sums, left, coupling, right_next, pack)

    coeff = jnp.zeros((HALF, 256), BF16)
    summed = jnp.zeros((leaf_count, 16, LANES), BF16)
    for turn in range(1, layer_count):
        early = ahead(sums, turn - 1, 0, 1 if turn == layer_count - 1 else 2)
        got = ahead(sent, turn - 1, 0)
        got_low = ahead(sent_up, turn - 1, 1)
        got_up = ahead(sent_low, turn - 1, -1)
        value, coeff, sent, sent_low, sent_up, sums = pl.pallas_call(
            functools.partial(turn_kernel, turn),
            out_shape=[shape((ROWS, width), F32), shape((HALF, 256), BF16), *field_shapes],
            in_specs=vmem(4) + anywhere(7), out_specs=anywhere(6),
            scratch_shapes=[
                pltpu.VMEM(slabs_shape, BF16), pltpu.VMEM((ROWS, width), BF16), pltpu.VMEM(base_shape, F32), pltpu.VMEM(weights_shape, BF16), pltpu.VMEM((ROWS, width), F32), pltpu.VMEM((HALF, 256), BF16),
                *[pltpu.VMEM(item.shape, item.dtype) for item in field_shapes], pltpu.SemaphoreType.DMA((leaves + 9,)),
            ],
            input_output_aliases={9: 0, 10: 1}, compiler_params=params, name="turn",
        )(got, got_low, got_up, summed, right_next, blocks, early, base, weights, value, coeff)
        summed = to_all_of(min(turn + 1, layer_count - 1), early)
    out = pl.pallas_call(
        functools.partial(last_kernel, layer_count),
        out_shape=shape((ROWS, width), BF16),
        in_specs=vmem(2) + anywhere(3), out_specs=vmem(1)[0],
        scratch_shapes=[
            pltpu.VMEM((ROWS, LANES), BF16), pltpu.VMEM((ROWS, width), F32), pltpu.VMEM((256, 2 * width), BF16),
            pltpu.SemaphoreType.DMA((3,)),
        ],
        compiler_params=params, name="last",
    )(back(coeff), summed, sent, value, left_w)
    return out.reshape(2, HALF, width)[None]


def solution(mesh):
    placed = (
        P("layer", None, None, "leaf"),
        P("layer", None, None, "leaf", None),
        P("layer", None, None, None, "leaf"),
        P("layer", None, None, None, "leaf"),
        P("layer", "leaf"),
        P("layer", None),
    )
    return jax.shard_map(
        body, mesh=mesh, in_specs=placed, out_specs=P("layer", None, None, "leaf"), check_vma=False
    )
```
